32 devices in a mesh: rep: 2 (over x), node: 2 (over core), local: 8 (over z, y).
Axes of the slice: x: 2, y: 2, z: 4, core: 2. Of those that a mesh axis runs over, the one named last changes fastest.
Arguments:
- head_outputs: bfloat16 [8192, 2560], P(('rep', 'node', 'local')), parts along dimension 0, may hold values from -6 to 6
- out_grads: bfloat16 [8192, 2560], P(('rep', 'node', 'local')), parts along dimension 0, may hold values from -6 to 6
- quant_values: bfloat16 [2560, 2560], P(('node', 'local')), may hold values from -0.125 to 0.125
- block_scales: bfloat16 [2560, 10], P(('node', 'local')), may hold values from 0.5 to 2
Outputs:
- projected: bfloat16 [8192, 2560], P(('rep', 'node', 'local')), parts along dimension 0
- head_grads: bfloat16 [8192, 2560], P(('rep', 'node', 'local')), parts along dimension 0
- weight_grad: float32 [5120, 2560], P(('rep', 'node', 'local')), parts along dimension 0
The draws below stay inside these ranges and needn't reach their ends.
There are 2 independent parts, one for each index of `rep`. The reference program is written for one: setup_inputs(seed, part) draws one part's arguments, and reference() takes and returns one part's arrays. A program takes and returns all parts, laid end to end along the dimension named above; an argument that names none is the same for every part. Nothing has to cross between parts.
All inputs are finite; a program needn't handle non-finite values.
Results may differ from the reference program's by a relative error of at most 0.005.
Values may be sent and summed in bfloat16 or wider, within the bound.
A program may use at most 192 MiB of HBM per device.

```python
import math
import jax
import jax.numpy as jnp
from jax import lax

TOK_DEV = 256
COLS = 2560
QBLOCK = 256
ROWS = 2560
TOKENS = 4096
N_NODE = 2
N_LOCAL = 8


def raised(drawn, own_key, source, target, blocks, factor):
    def block_of(axis_at):
        return (jnp.arange(drawn.shape[axis_at]) // (drawn.shape[axis_at] // blocks)).reshape((-1,) + (1,) * (drawn.ndim - 1 - axis_at))

    near = jax.random.permutation(own_key, blocks)[block_of(target)]
    other_side = (block_of(target) + blocks // 2) % blocks
    return jnp.where((block_of(source) == near) | (block_of(source) == other_side), factor * drawn, drawn)


def levels(own_key, extent, shards, least, top_value):
    level = 1.0
    for dim, blocks in shards:
        heights = jax.random.uniform(jax.random.fold_in(jax.random.fold_in(own_key, 6), dim), (blocks,), jnp.float32, least / len(shards), top_value / len(shards))
        level = level * jnp.repeat(jnp.exp(heights), extent[dim] // blocks).reshape((-1,) + (1,) * (len(extent) - 1 - dim))
    return level


def bell_draw(key, dims, width, most, split=(), kind=jnp.bfloat16):
    values = width * jax.random.normal(key, dims, jnp.float32)
    if split:
        values = values * levels(key, dims, split, -0.22, 0.18)
    return jnp.clip(values, -most, most).astype(kind)


def gaussian_with(own_key, dims, width, bound, cuts, heavy, held_as=jnp.bfloat16):
    result = width * jax.random.normal(own_key, dims, jnp.float32)
    if cuts:
        result = result * levels(own_key, dims, cuts, -0.22, 0.18)
    return jnp.clip(raised(result, jax.random.fold_in(own_key, 3), *heavy), -bound, bound).astype(held_as)


def setup_inputs(seed: int = 0, part: int = 0) -> dict:
    keys = jax.random.split(jax.random.key(seed), 5)
    part_splits = jax.random.split(jax.random.fold_in(keys[4], part), 5)
    return {
        "head_outputs": gaussian_with(part_splits[0], (TOKENS, ROWS), 1.0, 6.0, ((0, 16),), (0, 1, 16, 2.0)),
        "out_grads": bell_draw(part_splits[1], (TOKENS, COLS), 1.0, 6.0, ((0, 16),)),
        "quant_values": bell_draw(keys[2], (ROWS, COLS), ROWS ** -0.5, 0.125, ((0, 16),)),
        "block_scales": jnp.clip(jnp.exp(math.log(2.0) - 1.3862944 * jax.random.uniform(keys[3], (ROWS, COLS // QBLOCK), jnp.float32) ** levels(keys[3], (ROWS, COLS // QBLOCK), ((0, 16),), -0.2, 0.2)), 0.5, 2.0).astype(jnp.bfloat16),
    }


def dequantize(values, scales):
    row_count = values.shape[0]
    col_count = values.shape[1]
    blocks = scales.shape[1]
    widened = values.astype(jnp.float32).reshape(row_count, blocks, col_count // blocks)
    widened = widened * scales.astype(jnp.float32)[:, :, None]
    return widened.reshape(row_count, col_count).astype(jnp.bfloat16)


def reference(head_outputs, out_grads, quant_values, block_scales):
    weight = dequantize(quant_values, block_scales)
    projected = jnp.dot(head_outputs, weight, preferred_element_type=jnp.float32).astype(jnp.bfloat16)
    head_grads = lax.dot_general(out_grads, weight, (((1,), (1,)), ((), ())), preferred_element_type=jnp.float32).astype(jnp.bfloat16)
    head_blocks = head_outputs.reshape(N_NODE * N_LOCAL, TOK_DEV, ROWS)
    grad_blocks = out_grads.reshape(N_NODE * N_LOCAL, TOK_DEV, COLS)

    def accumulate(running, couple):
        product_term = lax.dot_general(couple[0], couple[1], (((0,), (0,)), ((), ())), preferred_element_type=jnp.float32)
        product_term = lax.optimization_barrier(product_term.astype(jnp.bfloat16)).astype(jnp.float32)
        return running + product_term, None

    initial = jnp.zeros((ROWS, COLS), jnp.float32)
    overall, _ = lax.scan(accumulate, initial, (head_blocks, grad_blocks))
    return projected, head_grads, overall * (TOKENS ** -0.5)
```

```python
import functools

import jax
import jax.numpy as jnp
from jax import lax
from jax.experimental import pallas as pl
from jax.experimental.pallas import tpu as pltpu
from jax.sharding import PartitionSpec as P


def dequantize(values, scales):
    row_count = values.shape[0]
    col_count = values.shape[1]
    blocks = scales.shape[1]
    widened = values.astype(jnp.float32).reshape(row_count, blocks, col_count // blocks)
    widened = widened * scales.astype(jnp.float32)[:, :, None]
    return widened.reshape(row_count, col_count).astype(jnp.bfloat16)


def fetch_weights(quant_values, block_scales):
    whole = (
        lax.all_gather(quant_values, ("node", "local"), axis=0, tiled=True),
        lax.all_gather(block_scales, ("node", "local"), axis=0, tiled=True),
    )
    values_all = whole[0]
    scales_all = whole[1]
    return dequantize(values_all, scales_all)


def apply_weight(weight, head_outputs, out_grads):
    projected = jnp.dot(head_outputs, weight, preferred_element_type=jnp.float32).astype(
        jnp.bfloat16
    )
    head_grads = lax.dot_general(
        out_grads, weight, (((1,), (1,)), ((), ())), preferred_element_type=jnp.float32
    ).astype(jnp.bfloat16)
    return (projected, head_grads)


def reduce_grads(head_outputs, out_grads, node_count, local_count):
    partial_value = lax.dot_general(
        head_outputs, out_grads, (((0,), (0,)), ((), ())), preferred_element_type=jnp.float32
    ).astype(jnp.bfloat16)
    col_count = partial_value.shape[1]
    shaped = partial_value.reshape(node_count, local_count, -1, col_count)
    arrived = lax.all_to_all(shaped, "local", split_axis=1, concat_axis=1, tiled=True)
    group_sum = jnp.sum(arrived, axis=1, dtype=jnp.float32)
    second = lax.all_to_all(group_sum, "node", split_axis=0, concat_axis=0, tiled=True)
    return jnp.sum(second, axis=0)


MESH = pl.DeviceIdType.MESH
CHUNKS = 4


def fused_kernel(
    scale, ho_ref, og_ref, ht_ref, qv_ref, sc_ref, proj_ref, hg_ref, wg_ref,
    w, htall, ogall, gsum, sbuf, f0, f1, ibuf, acc,
    hts, htr, ogys, ogyr, ogcs, ogcr, ogds, ogdr,
    wr, zs, ys, xs, cs, rss, f0r, f1r, ir,
):
    x = lax.axis_index("rep")
    c = lax.axis_index("node")
    l = lax.axis_index("local")
    z = l // 2
    y = l % 2
    xn, yn, cn = 1 - x, 1 - y, 1 - c
    side = z // 2
    pair = z + 1 - 2 * (z % 2)
    inner = 2 - side
    outer = 3 * (1 - side)
    is_inner = (z == 1) | (z == 2)
    shard = qv_ref.shape[0]
    half = shard // 2
    tok = ho_ref.shape[0]
    cols = og_ref.shape[1]
    cw = cols // CHUNKS

    def dev(xx, cc, zz, yy):
        return (xx, cc, zz * 2 + yy)

    to_x = dev(xn, c, z, y)
    to_y = dev(x, c, z, yn)
    to_c = dev(x, cn, z, y)
    to_d = dev(x, cn, z, yn)
    to_pair = dev(x, c, pair, y)
    to_inner = dev(x, c, inner, y)
    to_outer = dev(x, c, outer, y)

    barrier = pltpu.get_barrier_semaphore()
    for other in (to_x, to_y, to_c, to_d, to_pair, to_inner, to_outer):
        pl.semaphore_signal(barrier, inc=1, device_id=other, device_id_type=MESH)
    pl.semaphore_wait(barrier, 7)

    def rcopy(src, dst, ssem, rsem, to):
        return pltpu.make_async_remote_copy(
            src_ref=src, dst_ref=dst, send_sem=ssem, recv_sem=rsem,
            device_id=to, device_id_type=MESH,
        )

    def piece(zz, yy, hh, cc, ssem, to):
        row = pl.multiple_of(((cc * 8 + zz * 2 + yy) * 2 + hh) * half, half)
        at = w.at[pl.ds(row, half), :]
        return rcopy(at, at, ssem, wr.at[((cc * 4 + zz) * 2 + yy) * 2 + hh], to)

    started = []

    def send(copy):
        copy.start()
        started.append(copy)

    inner_started = []

    def arrive(zz, yy, hh, cc, sem, frm):
        piece(zz, yy, hh, cc, sem, frm).wait_recv()

    n_c = [0]

    def core_send(zz, yy, hh):
        send(piece(zz, yy, hh, c, cs.at[n_c[0]], to_c))
        n_c[0] += 1

    n_x = [0]

    def x_send(zz, yy):
        send(piece(zz, yy, x, c, xs.at[n_x[0]], to_x))
        n_x[0] += 1

    n_y = [0]

    def y_send(zz):
        send(piece(zz, y, x, c, ys.at[n_y[0]], to_y))
        n_y[0] += 1

    htc = {}
    for k, to, cc, yy in ((2, to_y, c, yn), (3, to_d, cn, yn), (1, to_c, cn, y)):
        htc[k] = rcopy(
            ht_ref.at[cc, yy], htall.at[:, pl.ds(k * tok, tok)], hts.at[k - 1], htr.at[k - 1], to
        )
        send(htc[k])

    ogall[0, 0:tok, :] = og_ref[:, 0:cw]

    def ogy(ch):
        return rcopy(
            ogall.at[ch, pl.ds(0, tok), :], ogall.at[ch, pl.ds(2 * tok, tok), :],
            ogys.at[ch], ogyr.at[ch], to_y,
        )

    def ogc(ch):
        return rcopy(
            ogall.at[ch, pl.ds(0, tok), :], ogall.at[ch, pl.ds(tok, tok), :],
            ogcs.at[ch], ogcr.at[ch], to_c,
        )

    def ogd(ch):
        return rcopy(
            ogall.at[ch, pl.ds(2 * tok, tok), :], ogall.at[ch, pl.ds(3 * tok, tok), :],
            ogds.at[ch], ogdr.at[ch], to_c,
        )

    send(ogy(0))

    own = pl.multiple_of((c * 8 + l) * shard, shard)
    qb = cols // sc_ref.shape[1]
    for b in range(sc_ref.shape[1]):
        w[pl.ds(own, shard), b * qb:(b + 1) * qb] = (
            qv_ref[:, b * qb:(b + 1) * qb].astype(jnp.float32)
            * sc_ref[:, b:b + 1].astype(jnp.float32)
        ).astype(jnp.bfloat16)

    send(piece(z, y, x, c, zs.at[0], to_pair))

    @pl.when(is_inner)
    def _():
        cp = piece(z, y, x, c, zs.at[1], to_inner)
        cp.start()
        inner_started.append(cp)

    for ch in range(1, CHUNKS):
        ogall[ch, 0:tok, :] = og_ref[:, ch * cw:(ch + 1) * cw]
    send(ogy(1))
    for ch in range(CHUNKS):
        send(ogc(ch))
    htall[:, 0:tok] = ht_ref[c, y]
    core_send(z, y, 0)
    core_send(z, y, 1)

    def z_step(zz, sem, to):
        arrive(zz, y, x, c, zs.at[0], to_pair)

        @pl.when(is_inner)
        def _():
            piece(zz, y, x, c, zs.at[sem], to).start()

        x_send(zz, y)
        core_send(zz, y, x)

    def grads(ch):
        ogy(ch).wait_recv()
        send(ogd(ch))
        if ch + 2 < CHUNKS:
            send(ogy(ch + 2))
        if ch == 0:
            for k in (1, 2, 3):
                htc[k].wait_recv()
        ogc(ch).wait_recv()
        ogd(ch).wait_recv()
        term = jnp.dot(htall[...], ogall[ch], preferred_element_type=jnp.float32)
        gsum[ch] = term.reshape(4, shard, cw)
        sbuf[ch, 0] = gsum[ch, pair].astype(jnp.bfloat16)
        send(rcopy(sbuf.at[ch, 0], f0.at[ch], rss.at[ch, 0], f0r.at[ch], to_pair))

        @pl.when(jnp.logical_not(is_inner))
        def _():
            for j, zz in ((1, inner), (2, outer)):
                sbuf[ch, j] = gsum[ch, zz].astype(jnp.bfloat16)
                rcopy(sbuf.at[ch, j], ibuf.at[ch, j - 1], rss.at[ch, j], ir.at[ch, j - 1], to_pair).start()

    def passed_on(ch):
        @pl.when(is_inner)
        def _():
            for j, zz, to in ((2, outer, to_outer), (1, inner, to_inner)):
                rcopy(sbuf.at[ch, j], ibuf.at[ch, j - 1], rss.at[ch, j], ir.at[ch, j - 1], to_pair).wait_recv()
                sbuf[ch, j] = (gsum[ch, zz] + ibuf[ch, j - 1].astype(jnp.float32)).astype(jnp.bfloat16)
                rcopy(sbuf.at[ch, j], f1.at[ch], rss.at[ch, j], f1r.at[ch], to).start()

    def finish(ch):
        rcopy(sbuf.at[ch, 0], f0.at[ch], rss.at[ch, 0], f0r.at[ch], to_pair).wait_recv()
        rcopy(sbuf.at[ch, 0], f1.at[ch], rss.at[ch, 0], f1r.at[ch], to_pair).wait_recv()
        wg_ref[:, ch * cw:(ch + 1) * cw] = (
            gsum[ch, z] + f0[ch].astype(jnp.float32) + f1[ch].astype(jnp.float32)
        ) * scale

    quarter = 4 * shard
    tile = cw

    def apply(cc, ss, first):
        row = pl.multiple_of((cc * 2 + ss) * quarter, 128)
        left = ho_ref[:, pl.ds(row, quarter)]

        def body(t, carry):
            at = pl.ds(pl.multiple_of(t * tile, 128), tile)
            term = jnp.dot(left, w[pl.ds(row, quarter), at], preferred_element_type=jnp.float32)
            if first:
                acc[:, at] = term
            else:
                acc[:, at] += term
            return carry

        lax.fori_loop(0, cols // tile, body, 0)
        hg_ref[:, pl.ds(row, quarter)] = lax.dot_general(
            og_ref[...], w[pl.ds(row, quarter), :], (((1,), (1,)), ((), ())),
            preferred_element_type=jnp.float32,
        ).astype(jnp.bfloat16)

    def b_step(zz):
        arrive(zz, yn, x, c, ys.at[0], to_y)
        x_send(zz, yn)
        core_send(zz, yn, x)

    def c_step(zz, yy):
        arrive(zz, yy, xn, c, xs.at[0], to_x)
        core_send(zz, yy, xn)

    def core_arrive(zz):
        for yy in (0, 1):
            for hh in (0, 1):
                arrive(zz, yy, hh, cn, cs.at[0], to_c)

    z_step(pair, 2, to_inner)
    z_step(inner, 3, to_pair)
    grads(0)
    z_step(outer, 4, to_pair)
    grads(1)
    passed_on(0)
    grads(2)
    y_send(z)
    y_send(pair)
    passed_on(1)
    grads(3)
    y_send(inner)
    y_send(outer)
    passed_on(2)
    c_step(pair, y)
    c_step(inner, y)
    c_step(outer, y)
    b_step(z)
    passed_on(3)
    b_step(pair)
    c_step(z, yn)
    b_step(inner)
    c_step(pair, yn)
    b_step(outer)
    apply(c, side, True)
    core_arrive(z)
    core_arrive(pair)
    apply(cn, side, False)
    c_step(inner, yn)
    c_step(outer, yn)
    for ch in range(CHUNKS):
        finish(ch)
    apply(c, 1 - side, False)
    core_arrive(inner)
    core_arrive(outer)
    apply(cn, 1 - side, False)
    proj_ref[...] = acc[...].astype(jnp.bfloat16)

    for copy in started:
        copy.wait_send()
    for ch in range(CHUNKS):
        for j in (1, 2):
            rcopy(sbuf.at[ch, j], f1.at[ch], rss.at[ch, j], f1r.at[ch], to_pair).wait_send()

    @pl.when(is_inner)
    def _():
        for k, zz in ((1, z), (2, pair), (3, inner), (4, outer)):
            piece(zz, y, x, c, zs.at[k], to_pair).wait_send()


def per_device_fused(head_outputs, out_grads, quant_values, block_scales):
    tok, rows = head_outputs.shape
    cols = out_grads.shape[1]
    shard = quant_values.shape[0]
    cw = cols // CHUNKS
    token_count = tok * lax.axis_size("node") * lax.axis_size("local")
    turned = head_outputs.T.reshape(2, 4, 2, shard, tok).transpose(0, 2, 1, 3, 4)
    turned = turned.reshape(2, 2, 4 * shard, tok)
    vmem = pl.BlockSpec(memory_space=pltpu.VMEM)
    bf16, f32 = jnp.bfloat16, jnp.float32
    dma = pltpu.SemaphoreType.DMA
    return pl.pallas_call(
        functools.partial(fused_kernel, token_count ** (-0.5)),
        out_shape=(
            jax.ShapeDtypeStruct((tok, cols), bf16),
            jax.ShapeDtypeStruct((tok, rows), bf16),
            jax.ShapeDtypeStruct((shard, cols), f32),
        ),
        in_specs=[vmem] * 5,
        out_specs=(vmem,) * 3,
        scratch_shapes=[
            pltpu.VMEM((rows, cols), bf16),
            pltpu.VMEM((4 * shard, 4 * tok), bf16),
            pltpu.VMEM((CHUNKS, 4 * tok, cw), bf16),
            pltpu.VMEM((CHUNKS, 4, shard, cw), f32),
            pltpu.VMEM((CHUNKS, 3, shard, cw), bf16),
            pltpu.VMEM((CHUNKS, shard, cw), bf16),
            pltpu.VMEM((CHUNKS, shard, cw), bf16),
            pltpu.VMEM((CHUNKS, 2, shard, cw), bf16),
            pltpu.VMEM((tok, cols), f32),
            dma((3,)), dma((3,)),
            dma((CHUNKS,)), dma((CHUNKS,)),
            dma((CHUNKS,)), dma((CHUNKS,)),
            dma((CHUNKS,)), dma((CHUNKS,)),
            dma((32,)), dma((5,)), dma((4,)), dma((7,)), dma((16,)),
            dma((CHUNKS, 3)), dma((CHUNKS,)), dma((CHUNKS,)), dma((CHUNKS, 2)),
        ],
        compiler_params=pltpu.CompilerParams(
            collective_id=0, has_side_effects=True, vmem_limit_bytes=60 * 1024 * 1024
        ),
        cost_estimate=pl.CostEstimate(
            flops=6 * tok * rows * cols, bytes_accessed=8 * tok * cols, transcendentals=0
        ),
    )(head_outputs, out_grads, turned, quant_values, block_scales)


def per_device_plain(head_outputs, out_grads, quant_values, block_scales):
    node_count = lax.axis_size("node")
    local_count = lax.axis_size("local")
    token_count = head_outputs.shape[0] * node_count * local_count
    weight = fetch_weights(quant_values, block_scales)
    projected, head_grads = apply_weight(weight, head_outputs, out_grads)
    reduced = reduce_grads(head_outputs, out_grads, node_count, local_count)
    return (projected, head_grads, reduced * token_count ** (-0.5))


def per_device(head_outputs, out_grads, quant_values, block_scales):
    node_count = lax.axis_size("node")
    local_count = lax.axis_size("local")
    shard = quant_values.shape[0]
    fits = (
        lax.axis_size("rep") == 2
        and node_count == 2
        and local_count == 8
        and shard % 32 == 0
        and (4 * shard) % 128 == 0
        and head_outputs.shape[0] % 256 == 0
        and out_grads.shape[1] % (CHUNKS * 128) == 0
    )
    if fits:
        return per_device_fused(head_outputs, out_grads, quant_values, block_scales)
    return per_device_plain(head_outputs, out_grads, quant_values, block_scales)


def solution(mesh):
    return jax.shard_map(
        per_device,
        mesh=mesh,
        in_specs=(
            P(("rep", "node", "local"), None),
            P(("rep", "node", "local"), None),
            P(("node", "local"), None),
            P(("node", "local"), None),
        ),
        out_specs=(
            P(("rep", "node", "local"), None),
            P(("rep", "node", "local"), None),
            P(("rep", "node", "local"), None),
        ),
        check_vma=False,
    )
```

```python
import functools

import jax
import jax.numpy as jnp
from jax import lax
from jax.experimental import pallas as pl
from jax.experimental.pallas import tpu as pltpu
from jax.sharding import PartitionSpec as P


def dequantize(values, scales):
    row_count = values.shape[0]
    col_count = values.shape[1]
    blocks = scales.shape[1]
    widened = values.astype(jnp.float32).reshape(row_count, blocks, col_count // blocks)
    widened = widened * scales.astype(jnp.float32)[:, :, None]
    return widened.reshape(row_count, col_count).astype(jnp.bfloat16)


def fetch_weights(quant_values, block_scales):
    whole = (
        lax.all_gather(quant_values, ("node", "local"), axis=0, tiled=True),
        lax.all_gather(block_scales, ("node", "local"), axis=0, tiled=True),
    )
    values_all = whole[0]
    scales_all = whole[1]
    return dequantize(values_all, scales_all)


def apply_weight(weight, head_outputs, out_grads):
    projected = jnp.dot(head_outputs, weight, preferred_element_type=jnp.float32).astype(
        jnp.bfloat16
    )
    head_grads = lax.dot_general(
        out_grads, weight, (((1,), (1,)), ((), ())), preferred_element_type=jnp.float32
    ).astype(jnp.bfloat16)
    return (projected, head_grads)


def reduce_grads(head_outputs, out_grads, node_count, local_count):
    partial_value = lax.dot_general(
        head_outputs, out_grads, (((0,), (0,)), ((), ())), preferred_element_type=jnp.float32
    ).astype(jnp.bfloat16)
    col_count = partial_value.shape[1]
    shaped = partial_value.reshape(node_count, local_count, -1, col_count)
    arrived = lax.all_to_all(shaped, "local", split_axis=1, concat_axis=1, tiled=True)
    group_sum = jnp.sum(arrived, axis=1, dtype=jnp.float32)
    second = lax.all_to_all(group_sum, "node", split_axis=0, concat_axis=0, tiled=True)
    return jnp.sum(second, axis=0)


MESH = pl.DeviceIdType.MESH
CHUNKS = 4


def fused_kernel(
    scale, ho_ref, og_ref, qv_ref, sc_ref, proj_ref, hg_ref, wg_ref,
    w, turned, htall, ogall, gsum, sbuf, f0, f1, ibuf, acc,
    hts, htr, ogys, ogyr, ogcs, ogcr, ogds, ogdr,
    wr, zs, ys, xs, cs, rss, f0r, f1r, ir,
):
    x = lax.axis_index("rep")
    c = lax.axis_index("node")
    l = lax.axis_index("local")
    z = l // 2
    y = l % 2
    xn, yn, cn = 1 - x, 1 - y, 1 - c
    side = z // 2
    pair = z + 1 - 2 * (z % 2)
    inner = 2 - side
    outer = 3 * (1 - side)
    is_inner = (z == 1) | (z == 2)
    shard = qv_ref.shape[0]
    half = shard // 2
    tok = ho_ref.shape[0]
    cols = og_ref.shape[1]
    cw = cols // CHUNKS

    def dev(xx, cc, zz, yy):
        return (xx, cc, zz * 2 + yy)

    to_x = dev(xn, c, z, y)
    to_y = dev(x, c, z, yn)
    to_c = dev(x, cn, z, y)
    to_d = dev(x, cn, z, yn)
    to_pair = dev(x, c, pair, y)
    to_inner = dev(x, c, inner, y)
    to_outer = dev(x, c, outer, y)

    barrier = pltpu.get_barrier_semaphore()
    for other in (to_x, to_y, to_c, to_d, to_pair, to_inner, to_outer):
        pl.semaphore_signal(barrier, inc=1, device_id=other, device_id_type=MESH)
    pl.semaphore_wait(barrier, 7)

    def rcopy(src, dst, ssem, rsem, to):
        return pltpu.make_async_remote_copy(
            src_ref=src, dst_ref=dst, send_sem=ssem, recv_sem=rsem,
            device_id=to, device_id_type=MESH,
        )

    def piece(zz, yy, hh, cc, ssem, to):
        row = pl.multiple_of(((cc * 8 + zz * 2 + yy) * 2 + hh) * half, half)
        at = w.at[pl.ds(row, half), :]
        return rcopy(at, at, ssem, wr.at[((cc * 4 + zz) * 2 + yy) * 2 + hh], to)

    started = []

    def send(copy):
        copy.start()
        started.append(copy)

    inner_started = []

    def arrive(zz, yy, hh, cc, sem, frm):
        piece(zz, yy, hh, cc, sem, frm).wait_recv()

    n_c = [0]

    def core_send(zz, yy, hh):
        send(piece(zz, yy, hh, c, cs.at[n_c[0]], to_c))
        n_c[0] += 1

    n_x = [0]

    def x_send(zz, yy):
        send(piece(zz, yy, x, c, xs.at[n_x[0]], to_x))
        n_x[0] += 1

    n_y = [0]

    def y_send(zz):
        send(piece(zz, y, x, c, ys.at[n_y[0]], to_y))
        n_y[0] += 1

    ogall[0, 0:tok, :] = og_ref[:, 0:cw]

    def ogy(ch):
        return rcopy(
            ogall.at[ch, pl.ds(0, tok), :], ogall.at[ch, pl.ds(2 * tok, tok), :],
            ogys.at[ch], ogyr.at[ch], to_y,
        )

    def ogc(ch):
        return rcopy(
            ogall.at[ch, pl.ds(0, tok), :], ogall.at[ch, pl.ds(tok, tok), :],
            ogcs.at[ch], ogcr.at[ch], to_c,
        )

    def ogd(ch):
        return rcopy(
            ogall.at[ch, pl.ds(2 * tok, tok), :], ogall.at[ch, pl.ds(3 * tok, tok), :],
            ogds.at[ch], ogdr.at[ch], to_c,
        )

    send(ogy(0))

    step = 256
    for b in range(ho_ref.shape[1] // step):
        turned[b * step:(b + 1) * step, :] = ho_ref[:, b * step:(b + 1) * step].T

    def ht_rows(cc, zz, yy):
        return pl.ds(pl.multiple_of((cc * 8 + zz * 2 + yy) * shard, shard), shard)

    htc = []
    for k, to, cc, yy in ((2, to_y, c, yn), (3, to_d, cn, yn), (1, to_c, cn, y)):
        for zz in range(4):
            htc.append(rcopy(
                turned.at[ht_rows(cc, zz, yy), :],
                htall.at[pl.ds(zz * shard, shard), pl.ds(k * tok, tok)],
                hts.at[k - 1, zz], htr.at[k - 1, zz], to,
            ))
            send(htc[-1])

    own = pl.multiple_of((c * 8 + l) * shard, shard)
    qb = cols // sc_ref.shape[1]
    for b in range(sc_ref.shape[1]):
        w[pl.ds(own, shard), b * qb:(b + 1) * qb] = (
            qv_ref[:, b * qb:(b + 1) * qb].astype(jnp.float32)
            * sc_ref[:, b:b + 1].astype(jnp.float32)
        ).astype(jnp.bfloat16)

    send(piece(z, y, x, c, zs.at[0], to_pair))

    @pl.when(is_inner)
    def _():
        cp = piece(z, y, x, c, zs.at[1], to_inner)
        cp.start()
        inner_started.append(cp)

    for ch in range(1, CHUNKS):
        ogall[ch, 0:tok, :] = og_ref[:, ch * cw:(ch + 1) * cw]
    for ch in range(CHUNKS):
        send(ogc(ch))
    for zz in range(4):
        htall[zz * shard:(zz + 1) * shard, 0:tok] = turned[ht_rows(c, zz, y), :]
    core_send(z, y, 0)
    core_send(z, y, 1)

    def z_step(zz, sem, to):
        arrive(zz, y, x, c, zs.at[0], to_pair)

        @pl.when(is_inner)
        def _():
            piece(zz, y, x, c, zs.at[sem], to).start()

        x_send(zz, y)
        core_send(zz, y, x)

    def grads(ch):
        ogy(ch).wait_recv()
        send(ogd(ch))
        if ch + 2 < CHUNKS:
            send(ogy(ch + 2))
        if ch == 0:
            for copy in htc:
                copy.wait_recv()
        ogc(ch).wait_recv()
        ogd(ch).wait_recv()
        term = jnp.dot(htall[...], ogall[ch], preferred_element_type=jnp.float32)
        gsum[ch] = term.reshape(4, shard, cw)
        sbuf[ch, 0] = gsum[ch, pair].astype(jnp.bfloat16)
        send(rcopy(sbuf.at[ch, 0], f0.at[ch], rss.at[ch, 0], f0r.at[ch], to_pair))

        @pl.when(jnp.logical_not(is_inner))
        def _():
            for j, zz in ((1, inner), (2, outer)):
                sbuf[ch, j] = gsum[ch, zz].astype(jnp.bfloat16)
                rcopy(sbuf.at[ch, j], ibuf.at[ch, j - 1], rss.at[ch, j], ir.at[ch, j - 1], to_pair).start()

    def passed_on(ch):
        @pl.when(is_inner)
        def _():
            for j, zz, to in ((2, outer, to_outer), (1, inner, to_inner)):
                rcopy(sbuf.at[ch, j], ibuf.at[ch, j - 1], rss.at[ch, j], ir.at[ch, j - 1], to_pair).wait_recv()
                sbuf[ch, j] = (gsum[ch, zz] + ibuf[ch, j - 1].astype(jnp.float32)).astype(jnp.bfloat16)
                rcopy(sbuf.at[ch, j], f1.at[ch], rss.at[ch, j], f1r.at[ch], to).start()

    def finish(ch):
        rcopy(sbuf.at[ch, 0], f0.at[ch], rss.at[ch, 0], f0r.at[ch], to_pair).wait_recv()
        rcopy(sbuf.at[ch, 0], f1.at[ch], rss.at[ch, 0], f1r.at[ch], to_pair).wait_recv()
        wg_ref[:, ch * cw:(ch + 1) * cw] = (
            gsum[ch, z] + f0[ch].astype(jnp.float32) + f1[ch].astype(jnp.float32)
        ) * scale

    quarter = 4 * shard
    tile = cw

    def apply(cc, ss, first):
        row = pl.multiple_of((cc * 2 + ss) * quarter, 128)
        left = ho_ref[:, pl.ds(row, quarter)]

        def body(t, carry):
            at = pl.ds(pl.multiple_of(t * tile, 128), tile)
            term = jnp.dot(left, w[pl.ds(row, quarter), at], preferred_element_type=jnp.float32)
            if first:
                acc[:, at] = term
            else:
                acc[:, at] += term
            return carry

        lax.fori_loop(0, cols // tile, body, 0)
        hg_ref[:, pl.ds(row, quarter)] = lax.dot_general(
            og_ref[...], w[pl.ds(row, quarter), :], (((1,), (1,)), ((), ())),
            preferred_element_type=jnp.float32,
        ).astype(jnp.bfloat16)

    def b_step(zz):
        arrive(zz, yn, x, c, ys.at[0], to_y)
        x_send(zz, yn)
        core_send(zz, yn, x)

    def c_step(zz, yy):
        arrive(zz, yy, xn, c, xs.at[0], to_x)
        core_send(zz, yy, xn)

    def core_arrive(zz):
        for yy in (0, 1):
            for hh in (0, 1):
                arrive(zz, yy, hh, cn, cs.at[0], to_c)

    z_step(pair, 2, to_inner)
    send(ogy(1))
    z_step(inner, 3, to_pair)
    grads(0)
    z_step(outer, 4, to_pair)
    grads(1)
    y_send(z)
    grads(2)
    y_send(pair)
    y_send(inner)
    grads(3)
    y_send(outer)
    c_step(pair, y)
    c_step(inner, y)
    c_step(outer, y)
    passed_on(0)
    b_step(z)
    b_step(pair)
    passed_on(1)
    c_step(z, yn)
    b_step(inner)
    c_step(pair, yn)
    apply(c, side, True)
    passed_on(2)
    b_step(outer)
    c_step(inner, yn)
    passed_on(3)
    core_arrive(z)
    core_arrive(pair)
    apply(cn, side, False)
    c_step(outer, yn)
    apply(c, 1 - side, False)
    core_arrive(inner)
    core_arrive(outer)
    apply(cn, 1 - side, False)
    for ch in range(CHUNKS):
        finish(ch)
    proj_ref[...] = acc[...].astype(jnp.bfloat16)

    for copy in started:
        copy.wait_send()
    for ch in range(CHUNKS):
        for j in (1, 2):
            rcopy(sbuf.at[ch, j], f1.at[ch], rss.at[ch, j], f1r.at[ch], to_pair).wait_send()

    @pl.when(is_inner)
    def _():
        for k, zz in ((1, z), (2, pair), (3, inner), (4, outer)):
            piece(zz, y, x, c, zs.at[k], to_pair).wait_send()


def per_device_fused(head_outputs, out_grads, quant_values, block_scales):
    tok, rows = head_outputs.shape
    cols = out_grads.shape[1]
    shard = quant_values.shape[0]
    cw = cols // CHUNKS
    token_count = tok * lax.axis_size("node") * lax.axis_size("local")
    vmem = pl.BlockSpec(memory_space=pltpu.VMEM)
    bf16, f32 = jnp.bfloat16, jnp.float32
    dma = pltpu.SemaphoreType.DMA
    return pl.pallas_call(
        functools.partial(fused_kernel, token_count ** (-0.5)),
        out_shape=(
            jax.ShapeDtypeStruct((tok, cols), bf16),
            jax.ShapeDtypeStruct((tok, rows), bf16),
            jax.ShapeDtypeStruct((shard, cols), f32),
        ),
        in_specs=[vmem] * 4,
        out_specs=(vmem,) * 3,
        scratch_shapes=[
            pltpu.VMEM((rows, cols), bf16),
            pltpu.VMEM((rows, tok), bf16),
            pltpu.VMEM((4 * shard, 4 * tok), bf16),
            pltpu.VMEM((CHUNKS, 4 * tok, cw), bf16),
            pltpu.VMEM((CHUNKS, 4, shard, cw), f32),
            pltpu.VMEM((CHUNKS, 3, shard, cw), bf16),
            pltpu.VMEM((CHUNKS, shard, cw), bf16),
            pltpu.VMEM((CHUNKS, shard, cw), bf16),
            pltpu.VMEM((CHUNKS, 2, shard, cw), bf16),
            pltpu.VMEM((tok, cols), f32),
            dma((3, 4)), dma((3, 4)),
            dma((CHUNKS,)), dma((CHUNKS,)),
            dma((CHUNKS,)), dma((CHUNKS,)),
            dma((CHUNKS,)), dma((CHUNKS,)),
            dma((32,)), dma((5,)), dma((4,)), dma((7,)), dma((16,)),
            dma((CHUNKS, 3)), dma((CHUNKS,)), dma((CHUNKS,)), dma((CHUNKS, 2)),
        ],
        compiler_params=pltpu.CompilerParams(
            collective_id=0, has_side_effects=True, vmem_limit_bytes=60 * 1024 * 1024
        ),
        cost_estimate=pl.CostEstimate(
            flops=6 * tok * rows * cols, bytes_accessed=8 * tok * cols, transcendentals=0
        ),
    )(head_outputs, out_grads, quant_values, block_scales)


def per_device_plain(head_outputs, out_grads, quant_values, block_scales):
    node_count = lax.axis_size("node")
    local_count = lax.axis_size("local")
    token_count = head_outputs.shape[0] * node_count * local_count
    weight = fetch_weights(quant_values, block_scales)
    projected, head_grads = apply_weight(weight, head_outputs, out_grads)
    reduced = reduce_grads(head_outputs, out_grads, node_count, local_count)
    return (projected, head_grads, reduced * token_count ** (-0.5))


def per_device(head_outputs, out_grads, quant_values, block_scales):
    node_count = lax.axis_size("node")
    local_count = lax.axis_size("local")
    shard = quant_values.shape[0]
    fits = (
        lax.axis_size("rep") == 2
        and node_count == 2
        and local_count == 8
        and shard % 32 == 0
        and (4 * shard) % 128 == 0
        and head_outputs.shape[0] % 256 == 0
        and head_outputs.shape[1] % 256 == 0
        and out_grads.shape[1] % (CHUNKS * 128) == 0
    )
    if fits:
        return per_device_fused(head_outputs, out_grads, quant_values, block_scales)
    return per_device_plain(head_outputs, out_grads, quant_values, block_scales)


def solution(mesh):
    return jax.shard_map(
        per_device,
        mesh=mesh,
        in_specs=(
            P(("rep", "node", "local"), None),
            P(("rep", "node", "local"), None),
            P(("node", "local"), None),
            P(("node", "local"), None),
        ),
        out_specs=(
            P(("rep", "node", "local"), None),
            P(("rep", "node", "local"), None),
            P(("rep", "node", "local"), None),
        ),
        check_vma=False,
    )
```

```python
import functools

import jax
import jax.numpy as jnp
from jax import lax
from jax.experimental import pallas as pl
from jax.experimental.pallas import tpu as pltpu
from jax.sharding import PartitionSpec as P


def dequantize(values, scales):
    row_count = values.shape[0]
    col_count = values.shape[1]
    blocks = scales.shape[1]
    widened = values.astype(jnp.float32).reshape(row_count, blocks, col_count // blocks)
    widened = widened * scales.astype(jnp.float32)[:, :, None]
    return widened.reshape(row_count, col_count).astype(jnp.bfloat16)


def fetch_weights(quant_values, block_scales):
    whole = (
        lax.all_gather(quant_values, ("node", "local"), axis=0, tiled=True),
        lax.all_gather(block_scales, ("node", "local"), axis=0, tiled=True),
    )
    values_all = whole[0]
    scales_all = whole[1]
    return dequantize(values_all, scales_all)


def apply_weight(weight, head_outputs, out_grads):
    projected = jnp.dot(head_outputs, weight, preferred_element_type=jnp.float32).astype(
        jnp.bfloat16
    )
    head_grads = lax.dot_general(
        out_grads, weight, (((1,), (1,)), ((), ())), preferred_element_type=jnp.float32
    ).astype(jnp.bfloat16)
    return (projected, head_grads)


def reduce_grads(head_outputs, out_grads, node_count, local_count):
    partial_value = lax.dot_general(
        head_outputs, out_grads, (((0,), (0,)), ((), ())), preferred_element_type=jnp.float32
    ).astype(jnp.bfloat16)
    col_count = partial_value.shape[1]
    shaped = partial_value.reshape(node_count, local_count, -1, col_count)
    arrived = lax.all_to_all(shaped, "local", split_axis=1, concat_axis=1, tiled=True)
    group_sum = jnp.sum(arrived, axis=1, dtype=jnp.float32)
    second = lax.all_to_all(group_sum, "node", split_axis=0, concat_axis=0, tiled=True)
    return jnp.sum(second, axis=0)


MESH = pl.DeviceIdType.MESH
CHUNKS = 4


def fused_kernel(
    scale, ho_ref, og_ref, qv_ref, sc_ref, proj_ref, hg_ref, wg_ref,
    w, turned, htall, ogall, gsum, sbuf, f0, f1, ibuf, acc,
    hts, htr, ogys, ogyr, ogcs, ogcr, ogds, ogdr,
    wr, zs, ys, xs, cs, rss, f0r, f1r, ir,
):
    x = lax.axis_index("rep")
    c = lax.axis_index("node")
    l = lax.axis_index("local")
    z = l // 2
    y = l % 2
    xn, yn, cn = 1 - x, 1 - y, 1 - c
    side = z // 2
    pair = z + 1 - 2 * (z % 2)
    inner = 2 - side
    outer = 3 * (1 - side)
    is_inner = (z == 1) | (z == 2)
    shard = qv_ref.shape[0]
    half = shard // 2
    tok = ho_ref.shape[0]
    cols = og_ref.shape[1]
    cw = cols // CHUNKS

    def dev(xx, cc, zz, yy):
        return (xx, cc, zz * 2 + yy)

    to_x = dev(xn, c, z, y)
    to_y = dev(x, c, z, yn)
    to_c = dev(x, cn, z, y)
    to_d = dev(x, cn, z, yn)
    to_pair = dev(x, c, pair, y)
    to_inner = dev(x, c, inner, y)
    to_outer = dev(x, c, outer, y)

    barrier = pltpu.get_barrier_semaphore()
    for other in (to_x, to_y, to_c, to_d, to_pair, to_inner, to_outer):
        pl.semaphore_signal(barrier, inc=1, device_id=other, device_id_type=MESH)
    pl.semaphore_wait(barrier, 7)

    def rcopy(src, dst, ssem, rsem, to):
        return pltpu.make_async_remote_copy(
            src_ref=src, dst_ref=dst, send_sem=ssem, recv_sem=rsem,
            device_id=to, device_id_type=MESH,
        )

    def piece(zz, yy, hh, cc, ssem, to):
        row = pl.multiple_of(((cc * 8 + zz * 2 + yy) * 2 + hh) * half, half)
        at = w.at[pl.ds(row, half), :]
        return rcopy(at, at, ssem, wr.at[((cc * 4 + zz) * 2 + yy) * 2 + hh], to)

    started = []

    def send(copy):
        copy.start()
        started.append(copy)

    inner_started = []

    def arrive(zz, yy, hh, cc, sem, frm):
        piece(zz, yy, hh, cc, sem, frm).wait_recv()

    n_c = [0]

    def core_send(zz, yy, hh):
        send(piece(zz, yy, hh, c, cs.at[n_c[0]], to_c))
        n_c[0] += 1

    n_x = [0]

    def x_send(zz, yy):
        send(piece(zz, yy, x, c, xs.at[n_x[0]], to_x))
        n_x[0] += 1

    n_y = [0]

    def y_send(zz):
        send(piece(zz, y, x, c, ys.at[n_y[0]], to_y))
        n_y[0] += 1

    ogall[0, 0:tok, :] = og_ref[:, 0:cw]

    def ogy(ch):
        return rcopy(
            ogall.at[ch, pl.ds(0, tok), :], ogall.at[ch, pl.ds(2 * tok, tok), :],
            ogys.at[ch], ogyr.at[ch], to_y,
        )

    def ogc(ch):
        return rcopy(
            ogall.at[ch, pl.ds(0, tok), :], ogall.at[ch, pl.ds(tok, tok), :],
            ogcs.at[ch], ogcr.at[ch], to_c,
        )

    def ogd(ch):
        return rcopy(
            ogall.at[ch, pl.ds(2 * tok, tok), :], ogall.at[ch, pl.ds(3 * tok, tok), :],
            ogds.at[ch], ogdr.at[ch], to_c,
        )

    send(ogy(0))

    step = 256
    for b in range(ho_ref.shape[1] // step):
        turned[b * step:(b + 1) * step, :] = ho_ref[:, b * step:(b + 1) * step].T

    def ht_rows(cc, zz, yy):
        return pl.ds(pl.multiple_of((cc * 8 + zz * 2 + yy) * shard, shard), shard)

    htc = []
    for k, to, cc, yy in ((2, to_y, c, yn), (3, to_d, cn, yn), (1, to_c, cn, y)):
        for zz in range(4):
            htc.append(rcopy(
                turned.at[ht_rows(cc, zz, yy), :],
                htall.at[pl.ds(zz * shard, shard), pl.ds(k * tok, tok)],
                hts.at[k - 1, zz], htr.at[k - 1, zz], to,
            ))
            send(htc[-1])

    own = pl.multiple_of((c * 8 + l) * shard, shard)
    blocks = sc_ref.shape[0]
    qb = cols // blocks
    hot = lax.broadcasted_iota(jnp.int32, (blocks, cols), 1) // qb
    hot = hot == lax.broadcasted_iota(jnp.int32, (blocks, cols), 0)
    factor = lax.dot_general(
        sc_ref[...].astype(jnp.float32).T.astype(jnp.bfloat16), hot.astype(jnp.bfloat16),
        (((1,), (0,)), ((), ())), preferred_element_type=jnp.float32,
    )
    w[pl.ds(own, shard), :] = (qv_ref[...].astype(jnp.float32) * factor).astype(jnp.bfloat16)

    send(piece(z, y, x, c, zs.at[0], to_pair))

    @pl.when(is_inner)
    def _():
        cp = piece(z, y, x, c, zs.at[1], to_inner)
        cp.start()
        inner_started.append(cp)

    for ch in range(1, CHUNKS):
        ogall[ch, 0:tok, :] = og_ref[:, ch * cw:(ch + 1) * cw]
    for ch in range(CHUNKS):
        send(ogc(ch))
    for zz in range(4):
        htall[zz * shard:(zz + 1) * shard, 0:tok] = turned[ht_rows(c, zz, y), :]
    core_send(z, y, 0)
    core_send(z, y, 1)

    def z_step(zz, sem, to):
        arrive(zz, y, x, c, zs.at[0], to_pair)

        @pl.when(is_inner)
        def _():
            piece(zz, y, x, c, zs.at[sem], to).start()

        x_send(zz, y)
        core_send(zz, y, x)

    def grads(ch):
        ogy(ch).wait_recv()
        send(ogd(ch))
        if ch + 2 < CHUNKS:
            send(ogy(ch + 2))
        if ch == 0:
            for copy in htc:
                copy.wait_recv()
        ogc(ch).wait_recv()
        ogd(ch).wait_recv()
        term = jnp.dot(htall[...], ogall[ch], preferred_element_type=jnp.float32)
        gsum[ch] = term.reshape(4, shard, cw)
        sbuf[ch, 0] = gsum[ch, pair].astype(jnp.bfloat16)
        send(rcopy(sbuf.at[ch, 0], f0.at[ch], rss.at[ch, 0], f0r.at[ch], to_pair))

        @pl.when(jnp.logical_not(is_inner))
        def _():
            for j, zz in ((1, inner), (2, outer)):
                sbuf[ch, j] = gsum[ch, zz].astype(jnp.bfloat16)
                rcopy(sbuf.at[ch, j], ibuf.at[ch, j - 1], rss.at[ch, j], ir.at[ch, j - 1], to_pair).start()

    def passed_on(ch):
        @pl.when(is_inner)
        def _():
            for j, zz, to in ((2, outer, to_outer), (1, inner, to_inner)):
                rcopy(sbuf.at[ch, j], ibuf.at[ch, j - 1], rss.at[ch, j], ir.at[ch, j - 1], to_pair).wait_recv()
                sbuf[ch, j] = (gsum[ch, zz] + ibuf[ch, j - 1].astype(jnp.float32)).astype(jnp.bfloat16)
                rcopy(sbuf.at[ch, j], f1.at[ch], rss.at[ch, j], f1r.at[ch], to).start()

    def finish(ch):
        rcopy(sbuf.at[ch, 0], f0.at[ch], rss.at[ch, 0], f0r.at[ch], to_pair).wait_recv()
        rcopy(sbuf.at[ch, 0], f1.at[ch], rss.at[ch, 0], f1r.at[ch], to_pair).wait_recv()
        wg_ref[:, ch * cw:(ch + 1) * cw] = (
            gsum[ch, z] + f0[ch].astype(jnp.float32) + f1[ch].astype(jnp.float32)
        ) * scale

    quarter = 4 * shard
    tile = cw

    def apply(cc, ss, first):
        row = pl.multiple_of((cc * 2 + ss) * quarter, 128)
        left = ho_ref[:, pl.ds(row, quarter)]

        def body(t, carry):
            at = pl.ds(pl.multiple_of(t * tile, 128), tile)
            term = jnp.dot(left, w[pl.ds(row, quarter), at], preferred_element_type=jnp.float32)
            if first:
                acc[:, at] = term
            else:
                acc[:, at] += term
            return carry

        lax.fori_loop(0, cols // tile, body, 0)
        hg_ref[:, pl.ds(row, quarter)] = lax.dot_general(
            og_ref[...], w[pl.ds(row, quarter), :], (((1,), (1,)), ((), ())),
            preferred_element_type=jnp.float32,
        ).astype(jnp.bfloat16)

    def b_step(zz):
        arrive(zz, yn, x, c, ys.at[0], to_y)
        x_send(zz, yn)
        core_send(zz, yn, x)

    def c_step(zz, yy):
        arrive(zz, yy, xn, c, xs.at[0], to_x)
        core_send(zz, yy, xn)

    def core_arrive(zz):
        for yy in (0, 1):
            for hh in (0, 1):
                arrive(zz, yy, hh, cn, cs.at[0], to_c)

    z_step(pair, 2, to_inner)
    send(ogy(1))
    z_step(inner, 3, to_pair)
    grads(0)
    z_step(outer, 4, to_pair)
    grads(1)
    y_send(z)
    grads(2)
    y_send(pair)
    y_send(inner)
    grads(3)
    y_send(outer)
    c_step(pair, y)
    c_step(inner, y)
    c_step(outer, y)
    passed_on(0)
    b_step(z)
    b_step(pair)
    passed_on(1)
    c_step(z, yn)
    b_step(inner)
    c_step(pair, yn)
    apply(c, side, True)
    passed_on(2)
    b_step(outer)
    c_step(inner, yn)
    core_arrive(z)
    core_arrive(pair)
    apply(cn, side, False)
    passed_on(3)
    finish(0)
    finish(1)
    c_step(outer, yn)
    finish(2)
    apply(c, 1 - side, False)
    core_arrive(inner)
    core_arrive(outer)
    apply(cn, 1 - side, False)
    finish(3)
    proj_ref[...] = acc[...].astype(jnp.bfloat16)

    for copy in started:
        copy.wait_send()
    for ch in range(CHUNKS):
        for j in (1, 2):
            rcopy(sbuf.at[ch, j], f1.at[ch], rss.at[ch, j], f1r.at[ch], to_pair).wait_send()

    @pl.when(is_inner)
    def _():
        for k, zz in ((1, z), (2, pair), (3, inner), (4, outer)):
            piece(zz, y, x, c, zs.at[k], to_pair).wait_send()


def per_device_fused(head_outputs, out_grads, quant_values, block_scales):
    tok, rows = head_outputs.shape
    cols = out_grads.shape[1]
    shard = quant_values.shape[0]
    cw = cols // CHUNKS
    token_count = tok * lax.axis_size("node") * lax.axis_size("local")
    vmem = pl.BlockSpec(memory_space=pltpu.VMEM)
    bf16, f32 = jnp.bfloat16, jnp.float32
    dma = pltpu.SemaphoreType.DMA
    return pl.pallas_call(
        functools.partial(fused_kernel, token_count ** (-0.5)),
        out_shape=(
            jax.ShapeDtypeStruct((tok, cols), bf16),
            jax.ShapeDtypeStruct((tok, rows), bf16),
            jax.ShapeDtypeStruct((shard, cols), f32),
        ),
        in_specs=[vmem] * 4,
        out_specs=(vmem,) * 3,
        scratch_shapes=[
            pltpu.VMEM((rows, cols), bf16),
            pltpu.VMEM((rows, tok), bf16),
            pltpu.VMEM((4 * shard, 4 * tok), bf16),
            pltpu.VMEM((CHUNKS, 4 * tok, cw), bf16),
            pltpu.VMEM((CHUNKS, 4, shard, cw), f32),
            pltpu.VMEM((CHUNKS, 3, shard, cw), bf16),
            pltpu.VMEM((CHUNKS, shard, cw), bf16),
            pltpu.VMEM((CHUNKS, shard, cw), bf16),
            pltpu.VMEM((CHUNKS, 2, shard, cw), bf16),
            pltpu.VMEM((tok, cols), f32),
            dma((3, 4)), dma((3, 4)),
            dma((CHUNKS,)), dma((CHUNKS,)),
            dma((CHUNKS,)), dma((CHUNKS,)),
            dma((CHUNKS,)), dma((CHUNKS,)),
            dma((32,)), dma((5,)), dma((4,)), dma((7,)), dma((16,)),
            dma((CHUNKS, 3)), dma((CHUNKS,)), dma((CHUNKS,)), dma((CHUNKS, 2)),
        ],
        compiler_params=pltpu.CompilerParams(
            collective_id=0, has_side_effects=True, vmem_limit_bytes=60 * 1024 * 1024
        ),
        cost_estimate=pl.CostEstimate(
            flops=6 * tok * rows * cols, bytes_accessed=8 * tok * cols, transcendentals=0
        ),
    )(head_outputs, out_grads, quant_values, block_scales.T)


def per_device_plain(head_outputs, out_grads, quant_values, block_scales):
    node_count = lax.axis_size("node")
    local_count = lax.axis_size("local")
    token_count = head_outputs.shape[0] * node_count * local_count
    weight = fetch_weights(quant_values, block_scales)
    projected, head_grads = apply_weight(weight, head_outputs, out_grads)
    reduced = reduce_grads(head_outputs, out_grads, node_count, local_count)
    return (projected, head_grads, reduced * token_count ** (-0.5))


def per_device(head_outputs, out_grads, quant_values, block_scales):
    node_count = lax.axis_size("node")
    local_count = lax.axis_size("local")
    shard = quant_values.shape[0]
    fits = (
        lax.axis_size("rep") == 2
        and node_count == 2
        and local_count == 8
        and shard % 32 == 0
        and (4 * shard) % 128 == 0
        and head_outputs.shape[0] % 256 == 0
        and head_outputs.shape[1] % 256 == 0
        and out_grads.shape[1] % (CHUNKS * 128) == 0
    )
    if fits:
        return per_device_fused(head_outputs, out_grads, quant_values, block_scales)
    return per_device_plain(head_outputs, out_grads, quant_values, block_scales)


def solution(mesh):
    return jax.shard_map(
        per_device,
        mesh=mesh,
        in_specs=(
            P(("rep", "node", "local"), None),
            P(("rep", "node", "local"), None),
            P(("node", "local"), None),
            P(("node", "local"), None),
        ),
        out_specs=(
            P(("rep", "node", "local"), None),
            P(("rep", "node", "local"), None),
            P(("rep", "node", "local"), None),
        ),
        check_vma=False,
    )
```

```python
import functools

import jax
import jax.numpy as jnp
from jax import lax
from jax.experimental import pallas as pl
from jax.experimental.pallas import tpu as pltpu
from jax.sharding import PartitionSpec as P


def dequantize(values, scales):
    row_count = values.shape[0]
    col_count = values.shape[1]
    blocks = scales.shape[1]
    widened = values.astype(jnp.float32).reshape(row_count, blocks, col_count // blocks)
    widened = widened * scales.astype(jnp.float32)[:, :, None]
    return widened.reshape(row_count, col_count).astype(jnp.bfloat16)


def fetch_weights(quant_values, block_scales):
    whole = (
        lax.all_gather(quant_values, ("node", "local"), axis=0, tiled=True),
        lax.all_gather(block_scales, ("node", "local"), axis=0, tiled=True),
    )
    values_all = whole[0]
    scales_all = whole[1]
    return dequantize(values_all, scales_all)


def apply_weight(weight, head_outputs, out_grads):
    projected = jnp.dot(head_outputs, weight, preferred_element_type=jnp.float32).astype(
        jnp.bfloat16
    )
    head_grads = lax.dot_general(
        out_grads, weight, (((1,), (1,)), ((), ())), preferred_element_type=jnp.float32
    ).astype(jnp.bfloat16)
    return (projected, head_grads)


def reduce_grads(head_outputs, out_grads, node_count, local_count):
    partial_value = lax.dot_general(
        head_outputs, out_grads, (((0,), (0,)), ((), ())), preferred_element_type=jnp.float32
    ).astype(jnp.bfloat16)
    col_count = partial_value.shape[1]
    shaped = partial_value.reshape(node_count, local_count, -1, col_count)
    arrived = lax.all_to_all(shaped, "local", split_axis=1, concat_axis=1, tiled=True)
    group_sum = jnp.sum(arrived, axis=1, dtype=jnp.float32)
    second = lax.all_to_all(group_sum, "node", split_axis=0, concat_axis=0, tiled=True)
    return jnp.sum(second, axis=0)


MESH = pl.DeviceIdType.MESH
CHUNKS = 4


def fused_kernel(
    scale, ho_ref, og_ref, qv_ref, sc_ref, proj_ref, hg_ref, wg_ref,
    w, turned, htall, ogall, gsum, sbuf, f0, f1, ibuf, acc,
    hts, htr, ogys, ogyr, ogcs, ogcr, ogds, ogdr,
    wr, zs, ys, xs, cs, rss, f0r, f1r, ir,
):
    x = lax.axis_index("rep")
    c = lax.axis_index("node")
    l = lax.axis_index("local")
    z = l // 2
    y = l % 2
    xn, yn, cn = 1 - x, 1 - y, 1 - c
    side = z // 2
    pair = z + 1 - 2 * (z % 2)
    inner = 2 - side
    outer = 3 * (1 - side)
    is_inner = (z == 1) | (z == 2)
    shard = qv_ref.shape[0]
    half = shard // 2
    tok = ho_ref.shape[0]
    cols = og_ref.shape[1]
    cw = cols // CHUNKS

    def dev(xx, cc, zz, yy):
        return (xx, cc, zz * 2 + yy)

    to_x = dev(xn, c, z, y)
    to_y = dev(x, c, z, yn)
    to_c = dev(x, cn, z, y)
    to_d = dev(x, cn, z, yn)
    to_pair = dev(x, c, pair, y)
    to_inner = dev(x, c, inner, y)
    to_outer = dev(x, c, outer, y)

    barrier = pltpu.get_barrier_semaphore()
    for other in (to_x, to_y, to_c, to_d, to_pair, to_inner, to_outer):
        pl.semaphore_signal(barrier, inc=1, device_id=other, device_id_type=MESH)
    pl.semaphore_wait(barrier, 7)

    def rcopy(src, dst, ssem, rsem, to):
        return pltpu.make_async_remote_copy(
            src_ref=src, dst_ref=dst, send_sem=ssem, recv_sem=rsem,
            device_id=to, device_id_type=MESH,
        )

    def piece(zz, yy, hh, cc, ssem, to):
        row = pl.multiple_of(((cc * 8 + zz * 2 + yy) * 2 + hh) * half, half)
        at = w.at[pl.ds(row, half), :]
        return rcopy(at, at, ssem, wr.at[((cc * 4 + zz) * 2 + yy) * 2 + hh], to)

    started = []

    def send(copy):
        copy.start()
        started.append(copy)

    inner_started = []

    def arrive(zz, yy, hh, cc, sem, frm):
        piece(zz, yy, hh, cc, sem, frm).wait_recv()

    n_c = [0]

    def core_send(zz, yy, hh):
        send(piece(zz, yy, hh, c, cs.at[n_c[0]], to_c))
        n_c[0] += 1

    n_x = [0]

    def x_send(zz, yy):
        send(piece(zz, yy, x, c, xs.at[n_x[0]], to_x))
        n_x[0] += 1

    n_y = [0]

    def y_send(zz):
        send(piece(zz, y, x, c, ys.at[n_y[0]], to_y))
        n_y[0] += 1

    ogall[0, 0:tok, :] = og_ref[:, 0:cw]

    def ogy(ch):
        return rcopy(
            ogall.at[ch, pl.ds(0, tok), :], ogall.at[ch, pl.ds(2 * tok, tok), :],
            ogys.at[ch], ogyr.at[ch], to_y,
        )

    def ogc(ch):
        return rcopy(
            ogall.at[ch, pl.ds(0, tok), :], ogall.at[ch, pl.ds(tok, tok), :],
            ogcs.at[ch], ogcr.at[ch], to_c,
        )

    def ogd(ch):
        return rcopy(
            ogall.at[ch, pl.ds(2 * tok, tok), :], ogall.at[ch, pl.ds(3 * tok, tok), :],
            ogds.at[ch], ogdr.at[ch], to_c,
        )

    send(ogy(0))

    step = 256
    for b in range(ho_ref.shape[1] // step):
        turned[b * step:(b + 1) * step, :] = ho_ref[:, b * step:(b + 1) * step].T

    def ht_rows(cc, zz, yy):
        return pl.ds(pl.multiple_of((cc * 8 + zz * 2 + yy) * shard, shard), shard)

    htc = []
    for k, to, cc, yy in ((2, to_y, c, yn), (3, to_d, cn, yn), (1, to_c, cn, y)):
        for zz in range(4):
            htc.append(rcopy(
                turned.at[ht_rows(cc, zz, yy), :],
                htall.at[pl.ds(zz * shard, shard), pl.ds(k * tok, tok)],
                hts.at[k - 1, zz], htr.at[k - 1, zz], to,
            ))
            send(htc[-1])

    own = pl.multiple_of((c * 8 + l) * shard, shard)
    blocks = sc_ref.shape[0]
    qb = cols // blocks
    hot = lax.broadcasted_iota(jnp.int32, (blocks, cols), 1) // qb
    hot = hot == lax.broadcasted_iota(jnp.int32, (blocks, cols), 0)
    factor = lax.dot_general(
        sc_ref[...].astype(jnp.float32).T.astype(jnp.bfloat16), hot.astype(jnp.bfloat16),
        (((1,), (0,)), ((), ())), preferred_element_type=jnp.float32,
    )
    w[pl.ds(own, shard), :] = (qv_ref[...].astype(jnp.float32) * factor).astype(jnp.bfloat16)

    send(piece(z, y, x, c, zs.at[0], to_pair))

    @pl.when(is_inner)
    def _():
        cp = piece(z, y, x, c, zs.at[1], to_inner)
        cp.start()
        inner_started.append(cp)

    for ch in range(1, CHUNKS):
        ogall[ch, 0:tok, :] = og_ref[:, ch * cw:(ch + 1) * cw]
    for ch in range(CHUNKS):
        send(ogc(ch))
    for zz in range(4):
        htall[zz * shard:(zz + 1) * shard, 0:tok] = turned[ht_rows(c, zz, y), :]
    core_send(z, y, 0)
    core_send(z, y, 1)

    def z_step(zz, sem, to):
        arrive(zz, y, x, c, zs.at[0], to_pair)

        @pl.when(is_inner)
        def _():
            piece(zz, y, x, c, zs.at[sem], to).start()

        x_send(zz, y)
        core_send(zz, y, x)

    def grads(ch):
        ogy(ch).wait_recv()
        send(ogd(ch))
        if ch + 2 < CHUNKS:
            send(ogy(ch + 2))
        if ch == 0:
            for copy in htc:
                copy.wait_recv()
        ogc(ch).wait_recv()
        ogd(ch).wait_recv()
        term = jnp.dot(htall[...], ogall[ch], preferred_element_type=jnp.float32)
        gsum[ch] = term.reshape(4, shard, cw)
        sbuf[ch, 0] = gsum[ch, pair].astype(jnp.bfloat16)
        send(rcopy(sbuf.at[ch, 0], f0.at[ch], rss.at[ch, 0], f0r.at[ch], to_pair))

        @pl.when(jnp.logical_not(is_inner))
        def _():
            for j, zz in ((1, inner), (2, outer)):
                sbuf[ch, j] = gsum[ch, zz].astype(jnp.bfloat16)
                rcopy(sbuf.at[ch, j], ibuf.at[ch, j - 1], rss.at[ch, j], ir.at[ch, j - 1], to_pair).start()

    def passed_on(ch):
        @pl.when(is_inner)
        def _():
            for j, zz, to in ((2, outer, to_outer), (1, inner, to_inner)):
                rcopy(sbuf.at[ch, j], ibuf.at[ch, j - 1], rss.at[ch, j], ir.at[ch, j - 1], to_pair).wait_recv()
                sbuf[ch, j] = (gsum[ch, zz] + ibuf[ch, j - 1].astype(jnp.float32)).astype(jnp.bfloat16)
                rcopy(sbuf.at[ch, j], f1.at[ch], rss.at[ch, j], f1r.at[ch], to).start()

    def finish(ch):
        rcopy(sbuf.at[ch, 0], f0.at[ch], rss.at[ch, 0], f0r.at[ch], to_pair).wait_recv()
        rcopy(sbuf.at[ch, 0], f1.at[ch], rss.at[ch, 0], f1r.at[ch], to_pair).wait_recv()
        wg_ref[:, ch * cw:(ch + 1) * cw] = (
            gsum[ch, z] + f0[ch].astype(jnp.float32) + f1[ch].astype(jnp.float32)
        ) * scale

    quarter = 4 * shard
    tile = cw

    def apply(cc, ss, first, last=False):
        row = pl.multiple_of((cc * 2 + ss) * quarter, 128)
        left = ho_ref[:, pl.ds(row, quarter)]

        def body(t, carry):
            at = pl.ds(pl.multiple_of(t * tile, 128), tile)
            term = jnp.dot(left, w[pl.ds(row, quarter), at], preferred_element_type=jnp.float32)
            if first:
                acc[:, at] = term
            elif last:
                proj_ref[:, at] = (acc[:, at] + term).astype(jnp.bfloat16)
            else:
                acc[:, at] += term
            return carry

        lax.fori_loop(0, cols // tile, body, 0)
        hg_ref[:, pl.ds(row, quarter)] = lax.dot_general(
            og_ref[...], w[pl.ds(row, quarter), :], (((1,), (1,)), ((), ())),
            preferred_element_type=jnp.float32,
        ).astype(jnp.bfloat16)

    def b_step(zz):
        arrive(zz, yn, x, c, ys.at[0], to_y)
        x_send(zz, yn)
        core_send(zz, yn, x)

    def c_step(zz, yy):
        arrive(zz, yy, xn, c, xs.at[0], to_x)
        core_send(zz, yy, xn)

    def core_arrive(zz):
        for yy in (0, 1):
            for hh in (0, 1):
                arrive(zz, yy, hh, cn, cs.at[0], to_c)

    z_step(pair, 2, to_inner)
    send(ogy(1))
    z_step(inner, 3, to_pair)
    grads(0)
    z_step(outer, 4, to_pair)
    grads(1)
    y_send(z)
    grads(2)
    y_send(pair)
    y_send(inner)
    grads(3)
    y_send(outer)
    c_step(pair, y)
    c_step(inner, y)
    c_step(outer, y)
    passed_on(0)
    b_step(z)
    b_step(pair)
    passed_on(1)
    c_step(z, yn)
    b_step(inner)
    c_step(pair, yn)
    apply(c, side, True)
    passed_on(2)
    b_step(outer)
    c_step(inner, yn)
    core_arrive(z)
    core_arrive(pair)
    apply(cn, side, False)
    passed_on(3)
    finish(0)
    finish(1)
    c_step(outer, yn)
    finish(2)
    apply(c, 1 - side, False)
    core_arrive(inner)
    core_arrive(outer)
    apply(cn, 1 - side, False, True)
    finish(3)

    for copy in started:
        copy.wait_send()
    for ch in range(CHUNKS):
        for j in (1, 2):
            rcopy(sbuf.at[ch, j], f1.at[ch], rss.at[ch, j], f1r.at[ch], to_pair).wait_send()

    @pl.when(is_inner)
    def _():
        for k, zz in ((1, z), (2, pair), (3, inner), (4, outer)):
            piece(zz, y, x, c, zs.at[k], to_pair).wait_send()


def per_device_fused(head_outputs, out_grads, quant_values, block_scales):
    tok, rows = head_outputs.shape
    cols = out_grads.shape[1]
    shard = quant_values.shape[0]
    cw = cols // CHUNKS
    token_count = tok * lax.axis_size("node") * lax.axis_size("local")
    vmem = pl.BlockSpec(memory_space=pltpu.VMEM)
    bf16, f32 = jnp.bfloat16, jnp.float32
    dma = pltpu.SemaphoreType.DMA
    return pl.pallas_call(
        functools.partial(fused_kernel, token_count ** (-0.5)),
        out_shape=(
            jax.ShapeDtypeStruct((tok, cols), bf16),
            jax.ShapeDtypeStruct((tok, rows), bf16),
            jax.ShapeDtypeStruct((shard, cols), f32),
        ),
        in_specs=[vmem] * 4,
        out_specs=(vmem,) * 3,
        scratch_shapes=[
            pltpu.VMEM((rows, cols), bf16),
            pltpu.VMEM((rows, tok), bf16),
            pltpu.VMEM((4 * shard, 4 * tok), bf16),
            pltpu.VMEM((CHUNKS, 4 * tok, cw), bf16),
            pltpu.VMEM((CHUNKS, 4, shard, cw), f32),
            pltpu.VMEM((CHUNKS, 3, shard, cw), bf16),
            pltpu.VMEM((CHUNKS, shard, cw), bf16),
            pltpu.VMEM((CHUNKS, shard, cw), bf16),
            pltpu.VMEM((CHUNKS, 2, shard, cw), bf16),
            pltpu.VMEM((tok, cols), f32),
            dma((3, 4)), dma((3, 4)),
            dma((CHUNKS,)), dma((CHUNKS,)),
            dma((CHUNKS,)), dma((CHUNKS,)),
            dma((CHUNKS,)), dma((CHUNKS,)),
            dma((32,)), dma((5,)), dma((4,)), dma((7,)), dma((16,)),
            dma((CHUNKS, 3)), dma((CHUNKS,)), dma((CHUNKS,)), dma((CHUNKS, 2)),
        ],
        compiler_params=pltpu.CompilerParams(
            collective_id=0, has_side_effects=True, vmem_limit_bytes=60 * 1024 * 1024
        ),
        cost_estimate=pl.CostEstimate(
            flops=6 * tok * rows * cols, bytes_accessed=8 * tok * cols, transcendentals=0
        ),
    )(head_outputs, out_grads, quant_values, block_scales.T)


def per_device_plain(head_outputs, out_grads, quant_values, block_scales):
    node_count = lax.axis_size("node")
    local_count = lax.axis_size("local")
    token_count = head_outputs.shape[0] * node_count * local_count
    weight = fetch_weights(quant_values, block_scales)
    projected, head_grads = apply_weight(weight, head_outputs, out_grads)
    reduced = reduce_grads(head_outputs, out_grads, node_count, local_count)
    return (projected, head_grads, reduced * token_count ** (-0.5))


def per_device(head_outputs, out_grads, quant_values, block_scales):
    node_count = lax.axis_size("node")
    local_count = lax.axis_size("local")
    shard = quant_values.shape[0]
    fits = (
        lax.axis_size("rep") == 2
        and node_count == 2
        and local_count == 8
        and shard % 32 == 0
        and (4 * shard) % 128 == 0
        and head_outputs.shape[0] % 256 == 0
        and head_outputs.shape[1] % 256 == 0
        and out_grads.shape[1] % (CHUNKS * 128) == 0
    )
    if fits:
        return per_device_fused(head_outputs, out_grads, quant_values, block_scales)
    return per_device_plain(head_outputs, out_grads, quant_values, block_scales)


def solution(mesh):
    return jax.shard_map(
        per_device,
        mesh=mesh,
        in_specs=(
            P(("rep", "node", "local"), None),
            P(("rep", "node", "local"), None),
            P(("node", "local"), None),
            P(("node", "local"), None),
        ),
        out_specs=(
            P(("rep", "node", "local"), None),
            P(("rep", "node", "local"), None),
            P(("rep", "node", "local"), None),
        ),
        check_vma=False,
    )
```
